512 devices in a mesh: dp: 64 (over y, z), feat: 8 (over x, core).
Axes of the slice: x: 4, y: 4, z: 16, core: 2. Of those that a mesh axis runs over, the one named last changes fastest.
Arguments:
- samples: bfloat16 [8192, 131072], P('dp', 'feat'), may hold values from -70 to 70
- estimates: bfloat16 [64, 8, 16384], P(None, 'feat', 'dp'), may hold values from -18 to 18
Outputs:
- updated: bfloat16 [64, 8, 16384], P(None, 'feat', 'dp')
The draws below stay inside these ranges and needn't reach their ends.
All inputs are finite; a program needn't handle non-finite values.
Results may differ from the reference program's by a relative error of at most 0.0095.
Values may be sent and summed in bfloat16 or wider, within the bound.
A program may use at most 64 MiB of HBM per device.

```python
import math
import jax
import jax.numpy as jnp
from jax import lax

F = 131072
K = 64
S = 8192
FEAT_BLOCKS = 8
BLOCK_FEATURES = 16384


def draw_samples(key, part):
    key = jax.random.fold_in(key, 1)
    keys = jax.random.split(key, 3)
    positions = jnp.arange(F, dtype=jnp.float32) / F
    feature_scale = jnp.exp(jax.random.uniform(keys[0], (F,), jnp.float32, math.log(0.35), math.log(2.8))) * (0.6 + 1.2 * positions)
    sample_scale = jnp.exp(jax.random.uniform(keys[1], (S,), jnp.float32, math.log(0.5), math.log(2.0)))
    base = jnp.clip(jax.random.normal(keys[2], (S, F), jnp.float32), -5.0, 5.0)
    values = sample_scale[:, None] * feature_scale[None, :] * base
    return values.astype(jnp.bfloat16)


def draw_estimates(key, part):
    key = jax.random.fold_in(key, 2)
    keys = jax.random.split(key, 4)
    noise = jnp.clip(jax.random.normal(keys[0], (K, F), jnp.float32), -5.0, 5.0)
    shared = jnp.clip(jax.random.normal(keys[1], (F,), jnp.float32), -4.0, 4.0)
    weights = jax.random.uniform(keys[2], (K,), jnp.float32, 0.4, 1.2)
    scales = jnp.exp(jax.random.uniform(keys[3], (K,), jnp.float32, math.log(0.6), math.log(1.8)))
    values = scales[:, None] * (noise + weights[:, None] * shared[None, :])
    return values.reshape(K, FEAT_BLOCKS, BLOCK_FEATURES).astype(jnp.bfloat16)


def setup_inputs(seed: int = 0) -> dict:
    key_of = jax.random.split(jax.random.key(seed), 3)
    samples = draw_samples(jax.random.fold_in(key_of[2], 71), 0)
    estimates = draw_estimates(jax.random.fold_in(key_of[2], 71), 0)
    return dict(samples=samples, estimates=estimates)


step_rate = 0.05
epsilon = 1e-06

def reference(samples, estimates):
    shaped = estimates.reshape(estimates.shape[0], -1)
    partial_value = lax.dot_general(shaped, samples, (((1,), (1,)), ((), ())), preferred_element_type=jnp.float32)
    scores = (partial_value * (1.0 / math.sqrt(F))).astype(jnp.bfloat16)
    total_samples = samples.shape[0]
    gram_matrix = lax.dot_general(scores, scores, (((1,), (1,)), ((), ())), preferred_element_type=jnp.float32) / total_samples
    product = jnp.dot(scores, samples, preferred_element_type=jnp.float32)
    current = shaped.astype(jnp.float32)
    penalty = jnp.tril(gram_matrix, -1)
    update_dir = math.sqrt(F) / total_samples * product - jnp.dot(penalty, current, precision=lax.Precision.HIGHEST)
    alignment = lax.optimization_barrier(jnp.mean(current * update_dir, axis=1))
    stepped = current + step_rate * (update_dir - alignment[:, None] * current)
    squares = lax.optimization_barrier(jnp.mean(stepped * stepped, axis=1))
    updated = stepped * lax.rsqrt(squares + epsilon)[:, None]
    return updated.astype(jnp.bfloat16).reshape(estimates.shape)
```

```python
import functools
import math

import jax
import jax.numpy as jnp
from jax import lax
from jax.experimental import pallas as pl
from jax.experimental.pallas import tpu as pltpu
from jax.sharding import PartitionSpec as P

F = 131072
STEP = 0.05
EPSILON = 1e-06
MESH = pl.DeviceIdType.MESH

NY, NZ, NF = 4, 16, 8
K = 64
ROWS = 128
WIDTH = 256
HALF = NZ // 2


def kernel(
    total_samples,
    x_hbm,
    u_ref,
    o_ref,
    x_v,
    gathered,
    score_slots,
    y_out,
    y_in,
    chain_out,
    chain_in,
    across_out,
    across_in,
    stat_z,
    stat_y,
    stat_f,
    x_sem,
    gather_send,
    gather_recv,
    score_send,
    score_recv,
    scatter_send,
    y_recv,
    chain_recv,
    across_recv,
    stat_send,
    stat_recv,
):
    dp = lax.axis_index("dp")
    feat = lax.axis_index("feat")
    y = dp // NZ
    z = dp % NZ
    up, down, across = (y + 1) % NY, (y + NY - 1) % NY, (y + 2) % NY

    def zof(offset):
        return (z + offset + NZ) % NZ

    right, left = zof(1), zof(-1)

    x_copy = pltpu.make_async_copy(x_hbm, x_v, x_sem)
    x_copy.start()

    barrier = pltpu.get_barrier_semaphore()
    partners = (
        [(dp // NZ * NZ + zof(i), feat) for i in range(1, NZ)]
        + [((y + i) % NY * NZ + z, feat) for i in range(1, NY)]
        + [(dp, (feat + i) % NF) for i in range(1, NF)]
    )
    for partner in partners:
        pl.semaphore_signal(barrier, inc=1, device_id=partner, device_id_type=MESH)
    pl.semaphore_wait(barrier, len(partners))

    def gather_copy(row, plane, to_row, to_plane, src=None):
        index = row * NZ + plane
        return pltpu.make_async_remote_copy(
            src_ref=gathered.at[index] if src is None else src,
            dst_ref=gathered.at[index],
            send_sem=gather_send,
            recv_sem=gather_recv.at[index],
            device_id=(to_row * NZ + to_plane, feat),
            device_id_type=MESH,
        )

    def arrived(row, plane):
        gather_copy(row, plane, y, right).wait_recv()

    for to_row, to_plane in ((y, right), (y, left), (across, z), (up, z), (down, z)):
        gather_copy(y, z, to_row, to_plane, u_ref).start()
    gathered[dp] = u_ref[...]

    def partial_scores(acc, row, plane):
        index = row * NZ + plane
        columns = pl.ds(pl.multiple_of(index * WIDTH, WIDTH), WIDTH)
        return acc + lax.dot_general(
            gathered[index],
            x_v[:, columns],
            (((1,), (1,)), ((), ())),
            preferred_element_type=jnp.float32,
        )

    arrived(across, z)
    gather_copy(across, z, y, right).start()
    gather_copy(across, z, y, left).start()
    x_copy.wait()
    acc = jnp.zeros((K, ROWS), jnp.float32)
    acc = partial_scores(acc, y, z)
    acc = partial_scores(acc, across, z)

    def gather_step(hop, acc, near, far_in, far_out):
        behind, ahead = zof(-hop), zof(hop)
        arrived(y, behind)
        if far_out:
            gather_copy(y, behind, y, right).start()
        gather_copy(y, behind, up, z).start()
        gather_copy(y, behind, down, z).start()
        arrived(across, ahead)
        if far_out:
            gather_copy(across, ahead, y, left).start()
        if near:
            arrived(y, ahead)
            if far_in:
                gather_copy(y, ahead, y, left).start()
            gather_copy(y, ahead, up, z).start()
            gather_copy(y, ahead, down, z).start()
            arrived(across, behind)
            if far_in:
                gather_copy(across, behind, y, right).start()
        acc = partial_scores(acc, y, behind)
        acc = partial_scores(acc, across, ahead)
        if near:
            acc = partial_scores(acc, y, ahead)
            acc = partial_scores(acc, across, behind)
        return acc

    def side_rows(acc, planes):
        for plane in planes:
            for row in (up, down):
                arrived(row, plane)
                acc = partial_scores(acc, row, plane)
        return acc

    acc = gather_step(1, acc, True, True, True)
    acc = side_rows(acc, (z,))

    def middle(hop, acc):
        acc = gather_step(hop, acc, True, True, True)
        return side_rows(acc, (zof(1 - hop), zof(hop - 1)))

    acc = lax.fori_loop(2, HALF - 1, middle, acc)
    acc = gather_step(HALF - 1, acc, True, False, True)
    acc = side_rows(acc, (zof(2 - HALF), zof(HALF - 2)))
    acc = gather_step(HALF, acc, False, False, False)
    acc = side_rows(acc, (zof(1 - HALF), zof(HALF - 1), zof(HALF)))

    score_slots[feat] = acc.astype(jnp.bfloat16)

    def score_copy(i):
        return pltpu.make_async_remote_copy(
            src_ref=score_slots.at[feat],
            dst_ref=score_slots.at[feat],
            send_sem=score_send,
            recv_sem=score_recv,
            device_id=(dp, (feat + i) % NF),
            device_id_type=MESH,
        )

    for i in range(1, NF):
        score_copy(i).start()
    seven = score_slots.at[pl.ds(0, NF - 1)]
    pltpu.make_async_copy(seven, seven, score_recv).wait()
    summed = score_slots[0].astype(jnp.float32)
    for i in range(1, NF):
        summed = summed + score_slots[i].astype(jnp.float32)
    scores = (summed * (1.0 / math.sqrt(F))).astype(jnp.bfloat16)

    gram = lax.dot_general(
        scores, scores, (((1,), (1,)), ((), ())), preferred_element_type=jnp.float32
    )
    below = lax.broadcasted_iota(jnp.int32, (K, K), 0) > lax.broadcasted_iota(
        jnp.int32, (K, K), 1
    )
    penalty = jnp.where(below, gram * (-1.0 / math.sqrt(F)), 0.0)
    high = penalty.astype(jnp.bfloat16)
    low = (penalty - high.astype(jnp.float32)).astype(jnp.bfloat16)
    weights = jnp.concatenate([scores, high, low], axis=1)

    def term(row, plane):
        index = row * NZ + plane
        columns = pl.ds(pl.multiple_of(index * WIDTH, WIDTH), WIDTH)
        shard = gathered[index]
        return jnp.dot(
            weights,
            jnp.concatenate([x_v[:, columns], shard, shard], axis=0),
            preferred_element_type=jnp.float32,
        )

    def side_copy(side, plane, to_row):
        return pltpu.make_async_remote_copy(
            src_ref=y_out.at[side, plane],
            dst_ref=y_in.at[side, plane],
            send_sem=scatter_send,
            recv_sem=y_recv.at[side, plane],
            device_id=(to_row * NZ + z, feat),
            device_id_type=MESH,
        )

    def send_sides(planes):
        for plane in planes:
            for side, row in ((0, up), (1, down)):
                y_out[side, plane] = term(row, plane).astype(jnp.bfloat16)
                side_copy(side, plane, row).start()

    def take_sides(total, plane):
        for side in (0, 1):
            side_copy(side, plane, up).wait_recv()
            total = total + y_in[side, plane].astype(jnp.float32)
        return total

    def chain_copy(lane, hop):
        return pltpu.make_async_remote_copy(
            src_ref=chain_out.at[lane, hop - 1],
            dst_ref=chain_in.at[lane, hop - 1],
            send_sem=scatter_send,
            recv_sem=chain_recv.at[lane, hop - 1],
            device_id=(y * NZ + (left if lane in (0, 3) else right), feat),
            device_id_type=MESH,
        )

    def take_chain(total, lane, hop):
        chain_copy(lane, hop + 1).wait_recv()
        return total + chain_in[lane, hop].astype(jnp.float32)

    def send_chain(total, lane, hop):
        chain_out[lane, hop - 1] = total.astype(jnp.bfloat16)
        chain_copy(lane, hop).start()

    def scatter_step(hop, lanes, heads, next_planes):
        behind, ahead = zof(-hop), zof(hop)
        send_sides(next_planes)
        where = {0: (y, behind), 1: (across, ahead), 2: (y, ahead), 3: (across, behind)}
        totals = {lane: term(*where[lane]) for lane in lanes}
        for lane in lanes:
            total = totals[lane]
            if lane in (0, 2):
                total = take_sides(total, where[lane][1])
            if lane not in heads:
                total = take_chain(total, lane, hop)
            send_chain(total, lane, hop)

    send_sides((zof(HALF),))
    scatter_step(HALF, (1, 0), (1, 0), (zof(1 - HALF), zof(HALF - 1)))
    scatter_step(HALF - 1, (1, 3, 0, 2), (3, 2), (zof(2 - HALF), zof(HALF - 2)))

    @pl.loop(0, HALF - 3)
    def _(i):
        hop = HALF - 2 - i
        scatter_step(hop, (1, 3, 0, 2), (), (zof(1 - hop), zof(hop - 1)))

    scatter_step(1, (1, 3, 0, 2), (), (z,))

    across_copy = pltpu.make_async_remote_copy(
        src_ref=across_out,
        dst_ref=across_in,
        send_sem=scatter_send,
        recv_sem=across_recv,
        device_id=(across * NZ + z, feat),
        device_id_type=MESH,
    )
    opposite = term(across, z)
    own = term(y, z)
    opposite = take_chain(take_chain(opposite, 1, 0), 3, 0)
    across_out[...] = opposite.astype(jnp.bfloat16)
    across_copy.start()
    own = take_sides(own, z)
    own = take_chain(take_chain(own, 0, 0), 2, 0)
    across_copy.wait_recv()
    own = own + across_in[...].astype(jnp.float32)

    current = u_ref[...].astype(jnp.float32)
    update = own * (math.sqrt(F) / total_samples)
    lane_of = lax.broadcasted_iota(jnp.int32, (K, 128), 1)
    stats = jnp.zeros((K, 128), jnp.float32)
    for lane, value in enumerate((current * current, current * update, update * update)):
        column = jnp.sum(value, axis=1, keepdims=True)
        stats = jnp.where(lane_of == lane, column, stats)
    stats = jnp.concatenate([stats, jnp.zeros_like(stats)], axis=0).T[:8]

    def total_over(stage, slots, me, count, device_of, value):
        slots[me] = value
        for i in range(1, count):
            pltpu.make_async_remote_copy(
                src_ref=slots.at[me],
                dst_ref=slots.at[me],
                send_sem=stat_send.at[stage],
                recv_sem=stat_recv.at[stage],
                device_id=device_of(i),
                device_id_type=MESH,
            ).start()
        others = slots.at[pl.ds(0, count - 1)]
        pltpu.make_async_copy(others, others, stat_recv.at[stage]).wait()
        total = slots[0]
        for i in range(1, count):
            total = total + slots[i]
        return total

    stats = total_over(0, stat_z, z, NZ, lambda i: (y * NZ + zof(i), feat), stats)
    stats = total_over(1, stat_y, y, NY, lambda i: ((y + i) % NY * NZ + z, feat), stats)
    stats = total_over(2, stat_f, feat, NF, lambda i: (dp, (feat + i) % NF), stats)

    columns = jnp.concatenate([stats, jnp.zeros((120, 128), jnp.float32)], axis=0).T[:K]
    columns = columns * (1.0 / F)
    alignment = columns[:, 1:2]
    keep = 1.0 - STEP * alignment
    squares = (
        keep * keep * columns[:, 0:1]
        + 2.0 * STEP * keep * alignment
        + STEP * STEP * columns[:, 2:3]
    )
    scale = lax.rsqrt(jnp.maximum(squares, 0.0) + EPSILON)
    o_ref[...] = ((keep * current + STEP * update) * scale).astype(jnp.bfloat16)

    sent = gathered.at[pl.ds(0, NY * NZ - 1)]
    pltpu.make_async_copy(sent, sent, gather_send).wait()
    pltpu.make_async_copy(seven, seven, score_send).wait()
    pltpu.make_async_copy(sent, sent, scatter_send).wait()
    for stage, (slots, count) in enumerate(((stat_z, NZ), (stat_y, NY), (stat_f, NF))):
        others = slots.at[pl.ds(0, count - 1)]
        pltpu.make_async_copy(others, others, stat_send.at[stage]).wait()


def shards(samples, estimates):
    shaped = estimates.reshape(K, WIDTH)
    total_samples = samples.shape[0] * lax.axis_size("dp")
    bf16, f32 = jnp.bfloat16, jnp.float32
    dma = pltpu.SemaphoreType.DMA
    updated = pl.pallas_call(
        functools.partial(kernel, total_samples),
        out_shape=jax.ShapeDtypeStruct((K, WIDTH), bf16),
        in_specs=[
            pl.BlockSpec(memory_space=pl.ANY),
            pl.BlockSpec(memory_space=pltpu.VMEM),
        ],
        out_specs=pl.BlockSpec(memory_space=pltpu.VMEM),
        scratch_shapes=[
            pltpu.VMEM((ROWS, NY * NZ * WIDTH), bf16),
            pltpu.VMEM((NY * NZ, K, WIDTH), bf16),
            pltpu.VMEM((NF, K, ROWS), bf16),
            pltpu.VMEM((2, NZ, K, WIDTH), bf16),
            pltpu.VMEM((2, NZ, K, WIDTH), bf16),
            pltpu.VMEM((4, HALF, K, WIDTH), bf16),
            pltpu.VMEM((4, HALF, K, WIDTH), bf16),
            pltpu.VMEM((K, WIDTH), bf16),
            pltpu.VMEM((K, WIDTH), bf16),
            pltpu.VMEM((NZ, 8, 128), f32),
            pltpu.VMEM((NY, 8, 128), f32),
            pltpu.VMEM((NF, 8, 128), f32),
            dma,
            dma,
            dma((NY * NZ,)),
            dma,
            dma,
            dma,
            dma((2, NZ)),
            dma((4, HALF)),
            dma,
            dma((3,)),
            dma((3,)),
        ],
        compiler_params=pltpu.CompilerParams(
            collective_id=0,
            has_side_effects=True,
            vmem_limit_bytes=48 * 1024 * 1024,
        ),
        cost_estimate=pl.CostEstimate(
            flops=4 * K * ROWS * NY * NZ * WIDTH,
            bytes_accessed=2 * ROWS * NY * NZ * WIDTH,
            transcendentals=0,
        ),
    )(samples, shaped)
    return updated.reshape(K, 1, WIDTH)


def solution(mesh):
    return jax.shard_map(
        shards,
        mesh=mesh,
        in_specs=(P("dp", "feat"), P(None, "feat", "dp")),
        out_specs=P(None, "feat", "dp"),
        check_vma=False,
    )
```

```python
import functools
import math

import jax
import jax.numpy as jnp
from jax import lax
from jax.experimental import pallas as pl
from jax.experimental.pallas import tpu as pltpu
from jax.sharding import PartitionSpec as P

F = 131072
STEP = 0.05
EPSILON = 1e-06
MESH = pl.DeviceIdType.MESH

NY, NZ, NF = 4, 16, 8
K = 64
ROWS = 128
WIDTH = 256
HALF = NZ // 2


def kernel(
    total_samples,
    x_hbm,
    u_hbm,
    o_ref,
    x_v,
    u_ref,
    gathered,
    score_slots,
    y_out,
    y_in,
    chain_out,
    chain_in,
    across_out,
    across_in,
    stat_z,
    stat_y,
    stat_f,
    x_sem,
    u_sem,
    gather_send,
    gather_recv,
    score_send,
    score_recv,
    scatter_send,
    y_recv,
    chain_recv,
    across_recv,
    stat_send,
    stat_recv,
):
    dp = lax.axis_index("dp")
    feat = lax.axis_index("feat")
    y = dp // NZ
    z = dp % NZ
    up, down, across = (y + 1) % NY, (y + NY - 1) % NY, (y + 2) % NY

    def zof(offset):
        return (z + offset + NZ) % NZ

    right, left = zof(1), zof(-1)

    x_copy = pltpu.make_async_copy(x_hbm, x_v, x_sem)
    u_copy = pltpu.make_async_copy(u_hbm, u_ref, u_sem)
    u_copy.start()
    x_copy.start()

    barrier = pltpu.get_barrier_semaphore()
    partners = (
        [(y * NZ + right, feat), (y * NZ + left, feat)]
        + [((y + i) % NY * NZ + z, feat) for i in range(1, NY)]
        + [(dp, (feat + i) % NF) for i in range(1, NF)]
    )
    for partner in partners:
        pl.semaphore_signal(barrier, inc=1, device_id=partner, device_id_type=MESH)
    u_copy.wait()
    pl.semaphore_wait(barrier, len(partners))

    def gather_copy(row, plane, to_row, to_plane, src=None):
        index = row * NZ + plane
        return pltpu.make_async_remote_copy(
            src_ref=gathered.at[index] if src is None else src,
            dst_ref=gathered.at[index],
            send_sem=gather_send,
            recv_sem=gather_recv.at[index],
            device_id=(to_row * NZ + to_plane, feat),
            device_id_type=MESH,
        )

    def arrived(row, plane):
        gather_copy(row, plane, y, right).wait_recv()

    for to_row, to_plane in ((y, right), (y, left), (across, z), (up, z), (down, z)):
        gather_copy(y, z, to_row, to_plane, u_ref).start()
    gathered[dp] = u_ref[...]

    def partial_scores(acc, row, plane):
        index = row * NZ + plane
        columns = pl.ds(pl.multiple_of(index * WIDTH, WIDTH), WIDTH)
        return acc + lax.dot_general(
            gathered[index],
            x_v[:, columns],
            (((1,), (1,)), ((), ())),
            preferred_element_type=jnp.float32,
        )

    arrived(across, z)
    gather_copy(across, z, y, right).start()
    gather_copy(across, z, y, left).start()
    x_copy.wait()
    acc = jnp.zeros((K, ROWS), jnp.float32)
    acc = partial_scores(acc, y, z)
    acc = partial_scores(acc, across, z)

    def gather_step(hop, acc, near, far_in, far_out):
        behind, ahead = zof(-hop), zof(hop)
        arrived(y, behind)
        if far_out:
            gather_copy(y, behind, y, right).start()
        gather_copy(y, behind, up, z).start()
        gather_copy(y, behind, down, z).start()
        arrived(across, ahead)
        if far_out:
            gather_copy(across, ahead, y, left).start()
        if near:
            arrived(y, ahead)
            if far_in:
                gather_copy(y, ahead, y, left).start()
            gather_copy(y, ahead, up, z).start()
            gather_copy(y, ahead, down, z).start()
            arrived(across, behind)
            if far_in:
                gather_copy(across, behind, y, right).start()
        acc = partial_scores(acc, y, behind)
        acc = partial_scores(acc, across, ahead)
        if near:
            acc = partial_scores(acc, y, ahead)
            acc = partial_scores(acc, across, behind)
        return acc

    def side_rows(acc, planes):
        for plane in planes:
            for row in (up, down):
                arrived(row, plane)
                acc = partial_scores(acc, row, plane)
        return acc

    acc = gather_step(1, acc, True, True, True)
    acc = side_rows(acc, (z,))

    def middle(hop, acc):
        acc = gather_step(hop, acc, True, True, True)
        return side_rows(acc, (zof(1 - hop), zof(hop - 1)))

    acc = lax.fori_loop(2, HALF - 1, middle, acc)
    acc = gather_step(HALF - 1, acc, True, False, True)
    acc = side_rows(acc, (zof(2 - HALF), zof(HALF - 2)))
    acc = gather_step(HALF, acc, False, False, False)
    acc = side_rows(acc, (zof(1 - HALF), zof(HALF - 1), zof(HALF)))

    score_slots[feat] = acc.astype(jnp.bfloat16)

    def score_copy(i):
        return pltpu.make_async_remote_copy(
            src_ref=score_slots.at[feat],
            dst_ref=score_slots.at[feat],
            send_sem=score_send,
            recv_sem=score_recv,
            device_id=(dp, (feat + i) % NF),
            device_id_type=MESH,
        )

    for i in range(1, NF):
        score_copy(i).start()
    seven = score_slots.at[pl.ds(0, NF - 1)]
    pltpu.make_async_copy(seven, seven, score_recv).wait()
    summed = score_slots[0].astype(jnp.float32)
    for i in range(1, NF):
        summed = summed + score_slots[i].astype(jnp.float32)
    scores = (summed * (1.0 / math.sqrt(F))).astype(jnp.bfloat16)

    gram = lax.dot_general(
        scores, scores, (((1,), (1,)), ((), ())), preferred_element_type=jnp.float32
    )
    below = lax.broadcasted_iota(jnp.int32, (K, K), 0) > lax.broadcasted_iota(
        jnp.int32, (K, K), 1
    )
    penalty = jnp.where(below, gram * (-1.0 / math.sqrt(F)), 0.0)
    high = penalty.astype(jnp.bfloat16)
    low = (penalty - high.astype(jnp.float32)).astype(jnp.bfloat16)
    weights = jnp.concatenate([scores, high, low], axis=1)

    def term(row, plane):
        index = row * NZ + plane
        columns = pl.ds(pl.multiple_of(index * WIDTH, WIDTH), WIDTH)
        shard = gathered[index]
        return jnp.dot(
            weights,
            jnp.concatenate([x_v[:, columns], shard, shard], axis=0),
            preferred_element_type=jnp.float32,
        )

    def side_copy(side, plane, to_row):
        return pltpu.make_async_remote_copy(
            src_ref=y_out.at[side, plane],
            dst_ref=y_in.at[side, plane],
            send_sem=scatter_send,
            recv_sem=y_recv.at[side, plane],
            device_id=(to_row * NZ + z, feat),
            device_id_type=MESH,
        )

    def send_sides(planes):
        for plane in planes:
            for side, row in ((0, up), (1, down)):
                y_out[side, plane] = term(row, plane).astype(jnp.bfloat16)
                side_copy(side, plane, row).start()

    def take_sides(total, plane):
        for side in (0, 1):
            side_copy(side, plane, up).wait_recv()
            total = total + y_in[side, plane].astype(jnp.float32)
        return total

    def chain_copy(lane, hop):
        return pltpu.make_async_remote_copy(
            src_ref=chain_out.at[lane, hop - 1],
            dst_ref=chain_in.at[lane, hop - 1],
            send_sem=scatter_send,
            recv_sem=chain_recv.at[lane, hop - 1],
            device_id=(y * NZ + (left if lane in (0, 3) else right), feat),
            device_id_type=MESH,
        )

    def take_chain(total, lane, hop):
        chain_copy(lane, hop + 1).wait_recv()
        return total + chain_in[lane, hop].astype(jnp.float32)

    def send_chain(total, lane, hop):
        chain_out[lane, hop - 1] = total.astype(jnp.bfloat16)
        chain_copy(lane, hop).start()

    def scatter_step(hop, lanes, heads, next_planes):
        behind, ahead = zof(-hop), zof(hop)
        send_sides(next_planes)
        where = {0: (y, behind), 1: (across, ahead), 2: (y, ahead), 3: (across, behind)}
        totals = {lane: term(*where[lane]) for lane in lanes}
        for lane in lanes:
            total = totals[lane]
            if lane in (0, 2):
                total = take_sides(total, where[lane][1])
            if lane not in heads:
                total = take_chain(total, lane, hop)
            send_chain(total, lane, hop)

    send_sides((zof(HALF),))
    scatter_step(HALF, (1, 0), (1, 0), (zof(1 - HALF), zof(HALF - 1)))
    scatter_step(HALF - 1, (1, 3, 0, 2), (3, 2), (zof(2 - HALF), zof(HALF - 2)))

    @pl.loop(0, HALF - 3)
    def _(i):
        hop = HALF - 2 - i
        scatter_step(hop, (1, 3, 0, 2), (), (zof(1 - hop), zof(hop - 1)))

    scatter_step(1, (1, 3, 0, 2), (), (z,))

    across_copy = pltpu.make_async_remote_copy(
        src_ref=across_out,
        dst_ref=across_in,
        send_sem=scatter_send,
        recv_sem=across_recv,
        device_id=(across * NZ + z, feat),
        device_id_type=MESH,
    )
    opposite = term(across, z)
    own = term(y, z)
    opposite = take_chain(take_chain(opposite, 1, 0), 3, 0)
    across_out[...] = opposite.astype(jnp.bfloat16)
    across_copy.start()
    own = take_sides(own, z)
    own = take_chain(take_chain(own, 0, 0), 2, 0)
    across_copy.wait_recv()
    own = own + across_in[...].astype(jnp.float32)

    current = u_ref[...].astype(jnp.float32)
    update = own * (math.sqrt(F) / total_samples)
    lane_of = lax.broadcasted_iota(jnp.int32, (K, 128), 1)
    stats = jnp.zeros((K, 128), jnp.float32)
    for lane, value in enumerate((current * current, current * update, update * update)):
        column = jnp.sum(value, axis=1, keepdims=True)
        stats = jnp.where(lane_of == lane, column, stats)
    stats = jnp.concatenate([stats, jnp.zeros_like(stats)], axis=0).T[:8]

    def total_over(stage, slots, me, count, device_of, value):
        slots[me] = value
        for i in sorted(range(1, count), key=lambda i: -min(i, count - i)):
            pltpu.make_async_remote_copy(
                src_ref=slots.at[me],
                dst_ref=slots.at[me],
                send_sem=stat_send.at[stage],
                recv_sem=stat_recv.at[stage],
                device_id=device_of(i),
                device_id_type=MESH,
            ).start()
        others = slots.at[pl.ds(0, count - 1)]
        pltpu.make_async_copy(others, others, stat_recv.at[stage]).wait()
        total = slots[0]
        for i in range(1, count):
            total = total + slots[i]
        return total

    stats = total_over(0, stat_z, z, NZ, lambda i: (y * NZ + zof(i), feat), stats)
    stats = total_over(1, stat_y, y, NY, lambda i: ((y + i) % NY * NZ + z, feat), stats)
    stats = total_over(2, stat_f, feat, NF, lambda i: (dp, (feat + i) % NF), stats)

    columns = jnp.concatenate([stats, jnp.zeros((120, 128), jnp.float32)], axis=0).T[:K]
    columns = columns * (1.0 / F)
    alignment = columns[:, 1:2]
    keep = 1.0 - STEP * alignment
    squares = (
        keep * keep * columns[:, 0:1]
        + 2.0 * STEP * keep * alignment
        + STEP * STEP * columns[:, 2:3]
    )
    scale = lax.rsqrt(jnp.maximum(squares, 0.0) + EPSILON)
    o_ref[...] = ((keep * current + STEP * update) * scale).astype(jnp.bfloat16)

    sent = gathered.at[pl.ds(0, NY * NZ - 1)]
    pltpu.make_async_copy(sent, sent, gather_send).wait()
    pltpu.make_async_copy(seven, seven, score_send).wait()
    pltpu.make_async_copy(sent, sent, scatter_send).wait()
    for stage, (slots, count) in enumerate(((stat_z, NZ), (stat_y, NY), (stat_f, NF))):
        others = slots.at[pl.ds(0, count - 1)]
        pltpu.make_async_copy(others, others, stat_send.at[stage]).wait()


def shards(samples, estimates):
    shaped = estimates.reshape(K, WIDTH)
    total_samples = samples.shape[0] * lax.axis_size("dp")
    bf16, f32 = jnp.bfloat16, jnp.float32
    dma = pltpu.SemaphoreType.DMA
    updated = pl.pallas_call(
        functools.partial(kernel, total_samples),
        out_shape=jax.ShapeDtypeStruct((K, WIDTH), bf16),
        in_specs=[
            pl.BlockSpec(memory_space=pl.ANY),
            pl.BlockSpec(memory_space=pl.ANY),
        ],
        out_specs=pl.BlockSpec(memory_space=pltpu.VMEM),
        scratch_shapes=[
            pltpu.VMEM((ROWS, NY * NZ * WIDTH), bf16),
            pltpu.VMEM((K, WIDTH), bf16),
            pltpu.VMEM((NY * NZ, K, WIDTH), bf16),
            pltpu.VMEM((NF, K, ROWS), bf16),
            pltpu.VMEM((2, NZ, K, WIDTH), bf16),
            pltpu.VMEM((2, NZ, K, WIDTH), bf16),
            pltpu.VMEM((4, HALF, K, WIDTH), bf16),
            pltpu.VMEM((4, HALF, K, WIDTH), bf16),
            pltpu.VMEM((K, WIDTH), bf16),
            pltpu.VMEM((K, WIDTH), bf16),
            pltpu.VMEM((NZ, 8, 128), f32),
            pltpu.VMEM((NY, 8, 128), f32),
            pltpu.VMEM((NF, 8, 128), f32),
            dma,
            dma,
            dma,
            dma((NY * NZ,)),
            dma,
            dma,
            dma,
            dma((2, NZ)),
            dma((4, HALF)),
            dma,
            dma((3,)),
            dma((3,)),
        ],
        compiler_params=pltpu.CompilerParams(
            collective_id=0,
            has_side_effects=True,
            vmem_limit_bytes=60 * 1024 * 1024,
        ),
        cost_estimate=pl.CostEstimate(
            flops=4 * K * ROWS * NY * NZ * WIDTH,
            bytes_accessed=2 * ROWS * NY * NZ * WIDTH,
            transcendentals=0,
        ),
    )(samples, shaped)
    return updated.reshape(K, 1, WIDTH)


def solution(mesh):
    return jax.shard_map(
        shards,
        mesh=mesh,
        in_specs=(P("dp", "feat"), P(None, "feat", "dp")),
        out_specs=P(None, "feat", "dp"),
        check_vma=False,
    )
```

```python
import functools
import math

import jax
import jax.numpy as jnp
from jax import lax
from jax.experimental import pallas as pl
from jax.experimental.pallas import tpu as pltpu
from jax.sharding import PartitionSpec as P

F = 131072
STEP = 0.05
EPSILON = 1e-06
MESH = pl.DeviceIdType.MESH
GROUP = 2
AHEAD = 2
ROOT = (0, 0)

NY, NZ, NF = 4, 16, 8
K = 64
ROWS = 128
WIDTH = 256

ARRIVALS = (
    (-1, 0), (1, 0), (0, 3), (0, -3), (2, 0), (0, 1), (0, -1), (-1, 1),
    (-1, -1), (1, -1), (-1, 3), (1, 3), (-1, -3), (1, -3), (0, 6), (2, 1),
    (1, 1), (0, -6), (0, 4), (2, -1), (0, -4), (0, -2), (2, 3), (-1, -2),
    (2, -3), (-1, 4), (-1, 2), (1, -2), (-1, -6), (2, 6), (0, 5), (0, 7),
    (-1, -4), (1, 6), (0, -7), (1, 2), (2, -2), (1, -6), (2, -4), (0, -5),
    (2, 2), (1, 4), (-1, -7), (2, 7), (2, -6), (0, 2), (2, 5), (1, 7),
    (-1, 5), (-1, 6), (0, 8), (1, -5), (1, -4), (1, -7), (2, -5), (-1, -5),
    (2, 4), (2, 8), (-1, 8), (1, 5), (-1, 7), (1, 8), (2, -7),
)
TARGETS = {
    (0, 0): ((0, 3), (0, -3), (-1, 0), (0, 1), (1, 0), (2, 0), (0, -1)),
    (-1, 0): ((-1, -1), (-1, 1)),
    (1, 0): ((1, -1),),
    (0, 3): ((0, 6), (0, 4), (-1, 3), (1, 3)),
    (0, -3): ((0, -6), (-1, -3), (0, -4), (1, -3), (0, -2)),
    (0, 1): ((1, 1),),
    (-1, 1): ((2, 1),),
    (-1, -1): ((-1, -2), (2, -1)),
    (-1, 3): ((-1, 2), (-1, 4)),
    (1, 3): ((2, 3),),
    (-1, -3): ((2, -3),),
    (1, -3): ((1, -2),),
    (0, 6): ((2, 6), (1, 6), (0, 5), (0, 7)),
    (1, 1): ((1, 2),),
    (0, -6): ((-1, -6), (0, -5), (0, -7), (1, -6)),
    (0, 4): ((1, 4),),
    (0, -4): ((-1, -4),),
    (-1, -2): ((2, -2),),
    (2, -3): ((2, -4),),
    (-1, 2): ((0, 2), (2, 2)),
    (-1, -6): ((2, -6), (-1, -7)),
    (2, 6): ((2, 5), (2, 7), (-1, 6)),
    (0, 5): ((-1, 5),),
    (1, 6): ((1, 7),),
    (0, -7): ((0, 8), (1, -7)),
    (1, -6): ((1, -5),),
    (2, -4): ((2, -5), (1, -4)),
    (0, -5): ((-1, -5),),
    (1, 4): ((2, 4),),
    (-1, -7): ((-1, 8),),
    (2, 7): ((2, 8), (-1, 7)),
    (2, -6): ((2, -7),),
    (2, 5): ((1, 5),),
    (1, 7): ((1, 8),),
}
NUMBER = {node: i for i, node in enumerate(ARRIVALS)}
COPIES = len(ARRIVALS)


def minus(a, b):
    dy, dz = (a[0] - b[0]) % NY, (a[1] - b[1]) % NZ
    return dy if dy <= NY // 2 else dy - NY, dz if dz <= NZ // 2 else dz - NZ


MOVES = sorted(
    {
        way
        for node, targets in TARGETS.items()
        for target in targets
        for way in (minus(target, node), minus(node, target))
    }
)


def kernel(
    total_samples,
    x_hbm,
    u_hbm,
    o_ref,
    x_v,
    u_ref,
    gathered,
    score_slots,
    scatter_out,
    scatter_in,
    stat_z,
    stat_y,
    stat_f,
    x_sem,
    u_sem,
    gather_send,
    gather_recv,
    score_send,
    score_recv,
    scatter_send,
    scatter_recv,
    stat_send,
    stat_recv,
):
    dp = lax.axis_index("dp")
    feat = lax.axis_index("feat")
    y = lax.div(dp, NZ)
    z = lax.rem(dp, NZ)

    def peer(dy, dz):
        return lax.rem(y + (dy + NY), NY) * NZ + lax.rem(z + (dz + NZ), NZ)

    def origin(node):
        return peer(-node[0], -node[1])

    def feat_peer(i):
        return lax.rem(feat + i, NF)

    x_copy = pltpu.make_async_copy(x_hbm, x_v, x_sem)
    u_copy = pltpu.make_async_copy(u_hbm, u_ref, u_sem)
    u_copy.start()
    x_copy.start()

    barrier = pltpu.get_barrier_semaphore()
    partners = [(peer(*way), feat) for way in MOVES]
    partners += [(dp, feat_peer(i)) for i in range(1, NF)]
    for partner in partners:
        pl.semaphore_signal(barrier, inc=1, device_id=partner, device_id_type=MESH)
    u_copy.wait()
    pl.semaphore_wait(barrier, len(partners))

    def gather_copy(node, target, src=None):
        index = origin(node)
        return pltpu.make_async_remote_copy(
            src_ref=gathered.at[index] if src is None else src,
            dst_ref=gathered.at[index],
            send_sem=gather_send,
            recv_sem=gather_recv.at[NUMBER[target]],
            device_id=(peer(*minus(target, node)), feat),
            device_id_type=MESH,
        )

    def arrived(node):
        shard = gathered.at[origin(node)]
        pltpu.make_async_copy(shard, shard, gather_recv.at[NUMBER[node]]).wait()

    for target in TARGETS[ROOT]:
        gather_copy(ROOT, target, u_ref).start()
    gathered[dp] = u_ref[...]

    def columns_of(index):
        return pl.ds(pl.multiple_of(index * WIDTH, WIDTH), WIDTH)

    def partial_scores(acc, nodes):
        for node in nodes:
            index = origin(node)
            acc = acc + lax.dot_general(
                gathered[index],
                x_v[:, columns_of(index)],
                (((1,), (1,)), ((), ())),
                preferred_element_type=jnp.float32,
            )
        return acc

    x_copy.wait()
    acc = partial_scores(jnp.zeros((K, ROWS), jnp.float32), (ROOT,))
    for start in range(0, COPIES, GROUP):
        group = ARRIVALS[start : start + GROUP]
        for node in group:
            arrived(node)
            for target in TARGETS.get(node, ()):
                gather_copy(node, target).start()
        acc = partial_scores(acc, group)

    score_slots[feat] = acc.astype(jnp.bfloat16)

    def score_copy(i):
        return pltpu.make_async_remote_copy(
            src_ref=score_slots.at[feat],
            dst_ref=score_slots.at[feat],
            send_sem=score_send,
            recv_sem=score_recv,
            device_id=(dp, feat_peer(i)),
            device_id_type=MESH,
        )

    for i in range(1, NF):
        score_copy(i).start()
    seven = score_slots.at[pl.ds(0, NF - 1)]
    pltpu.make_async_copy(seven, seven, score_recv).wait()
    summed = score_slots[0].astype(jnp.float32)
    for i in range(1, NF):
        summed = summed + score_slots[i].astype(jnp.float32)
    scores = (summed * (1.0 / math.sqrt(F))).astype(jnp.bfloat16)

    gram = lax.dot_general(
        scores, scores, (((1,), (1,)), ((), ())), preferred_element_type=jnp.float32
    )
    below = lax.broadcasted_iota(jnp.int32, (K, K), 0) > lax.broadcasted_iota(
        jnp.int32, (K, K), 1
    )
    penalty = jnp.where(below, gram * (-1.0 / math.sqrt(F)), 0.0)
    high = penalty.astype(jnp.bfloat16)
    low = (penalty - high.astype(jnp.float32)).astype(jnp.bfloat16)
    weights = jnp.concatenate([scores, high, low], axis=1)

    def term(node):
        index = origin(node)
        shard = gathered[index]
        return jnp.dot(
            weights,
            jnp.concatenate([x_v[:, columns_of(index)], shard, shard], axis=0),
            preferred_element_type=jnp.float32,
        )

    def scatter_copy(node, target):
        slot = NUMBER[target]
        return pltpu.make_async_remote_copy(
            src_ref=scatter_out.at[slot],
            dst_ref=scatter_in.at[slot],
            send_sem=scatter_send,
            recv_sem=scatter_recv.at[slot],
            device_id=(peer(*minus(node, target)), feat),
            device_id_type=MESH,
        )

    def take(total, node):
        for target in reversed(TARGETS.get(node, ())):
            slot = NUMBER[target]
            pltpu.make_async_copy(
                scatter_in.at[slot], scatter_in.at[slot], scatter_recv.at[slot]
            ).wait()
            total = total + scatter_in[slot].astype(jnp.float32)
        return total

    sources = {target: node for node, targets in TARGETS.items() for target in targets}
    departures = ARRIVALS[::-1] + (ROOT,)
    terms = [term(node) for node in departures[:AHEAD]]
    for i, node in enumerate(departures):
        if i + AHEAD < len(departures):
            terms.append(term(departures[i + AHEAD]))
        total = take(terms.pop(0), node)
        if node != ROOT:
            scatter_out[NUMBER[node]] = total.astype(jnp.bfloat16)
            scatter_copy(sources[node], node).start()
    own = total

    current = u_ref[...].astype(jnp.float32)
    update = own * (math.sqrt(F) / total_samples)
    lane_of = lax.broadcasted_iota(jnp.int32, (K, 128), 1)
    stats = jnp.zeros((K, 128), jnp.float32)
    for lane, value in enumerate((current * current, current * update, update * update)):
        column = jnp.sum(value, axis=1, keepdims=True)
        stats = jnp.where(lane_of == lane, column, stats)
    stats = jnp.concatenate([stats, jnp.zeros_like(stats)], axis=0).T[:8]

    def total_over(stage, slots, me, count, device_of, value):
        slots[me] = value
        for i in sorted(range(1, count), key=lambda i: -min(i, count - i)):
            pltpu.make_async_remote_copy(
                src_ref=slots.at[me],
                dst_ref=slots.at[me],
                send_sem=stat_send.at[stage],
                recv_sem=stat_recv.at[stage],
                device_id=device_of(i),
                device_id_type=MESH,
            ).start()
        others = slots.at[pl.ds(0, count - 1)]
        pltpu.make_async_copy(others, others, stat_recv.at[stage]).wait()
        total = slots[0]
        for i in range(1, count):
            total = total + slots[i]
        return total

    stats = total_over(0, stat_z, z, NZ, lambda i: (peer(0, i), feat), stats)
    stats = total_over(1, stat_y, y, NY, lambda i: (peer(i, 0), feat), stats)
    stats = total_over(2, stat_f, feat, NF, lambda i: (dp, feat_peer(i)), stats)

    columns = jnp.concatenate([stats, jnp.zeros((120, 128), jnp.float32)], axis=0).T[:K]
    columns = columns * (1.0 / F)
    alignment = columns[:, 1:2]
    keep = 1.0 - STEP * alignment
    squares = (
        keep * keep * columns[:, 0:1]
        + 2.0 * STEP * keep * alignment
        + STEP * STEP * columns[:, 2:3]
    )
    scale = lax.rsqrt(jnp.maximum(squares, 0.0) + EPSILON)
    o_ref[...] = ((keep * current + STEP * update) * scale).astype(jnp.bfloat16)

    sent = gathered.at[pl.ds(0, COPIES)]
    pltpu.make_async_copy(sent, sent, gather_send).wait()
    pltpu.make_async_copy(seven, seven, score_send).wait()
    pltpu.make_async_copy(sent, sent, scatter_send).wait()
    for stage, (slots, count) in enumerate(((stat_z, NZ), (stat_y, NY), (stat_f, NF))):
        others = slots.at[pl.ds(0, count - 1)]
        pltpu.make_async_copy(others, others, stat_send.at[stage]).wait()


def shards(samples, estimates):
    shaped = estimates.reshape(K, WIDTH)
    total_samples = samples.shape[0] * lax.axis_size("dp")
    bf16, f32 = jnp.bfloat16, jnp.float32
    dma = pltpu.SemaphoreType.DMA
    updated = pl.pallas_call(
        functools.partial(kernel, total_samples),
        out_shape=jax.ShapeDtypeStruct((K, WIDTH), bf16),
        in_specs=[
            pl.BlockSpec(memory_space=pl.ANY),
            pl.BlockSpec(memory_space=pl.ANY),
        ],
        out_specs=pl.BlockSpec(memory_space=pltpu.VMEM),
        scratch_shapes=[
            pltpu.VMEM((ROWS, NY * NZ * WIDTH), bf16),
            pltpu.VMEM((K, WIDTH), bf16),
            pltpu.VMEM((NY * NZ, K, WIDTH), bf16),
            pltpu.VMEM((NF, K, ROWS), bf16),
            pltpu.VMEM((COPIES, K, WIDTH), bf16),
            pltpu.VMEM((COPIES, K, WIDTH), bf16),
            pltpu.VMEM((NZ, 8, 128), f32),
            pltpu.VMEM((NY, 8, 128), f32),
            pltpu.VMEM((NF, 8, 128), f32),
            dma,
            dma,
            dma,
            dma((COPIES,)),
            dma,
            dma,
            dma,
            dma((COPIES,)),
            dma((3,)),
            dma((3,)),
        ],
        compiler_params=pltpu.CompilerParams(
            collective_id=0,
            has_side_effects=True,
            vmem_limit_bytes=60 * 1024 * 1024,
        ),
        cost_estimate=pl.CostEstimate(
            flops=4 * K * ROWS * NY * NZ * WIDTH,
            bytes_accessed=2 * ROWS * NY * NZ * WIDTH,
            transcendentals=0,
        ),
    )(samples, shaped)
    return updated.reshape(K, 1, WIDTH)


def solution(mesh):
    return jax.shard_map(
        shards,
        mesh=mesh,
        in_specs=(P("dp", "feat"), P(None, "feat", "dp")),
        out_specs=P(None, "feat", "dp"),
        check_vma=False,
    )
```

```python
import functools
import math

import jax
import jax.numpy as jnp
from jax import lax
from jax.experimental import pallas as pl
from jax.experimental.pallas import tpu as pltpu
from jax.sharding import PartitionSpec as P

F = 131072
STEP = 0.05
EPSILON = 1e-06
MESH = pl.DeviceIdType.MESH
GROUP = 2
AHEAD = 3
ROOT = (0, 0)

NY, NZ, NF = 4, 16, 8
K = 64
ROWS = 128
WIDTH = 256

ARRIVALS = (
    (-1, 0), (0, -2), (1, 0), (2, 0), (0, 3), (0, 1), (0, -3), (-1, 1),
    (0, -1), (-1, -2), (1, -2), (1, 3), (-1, 3), (1, 1), (-1, -3), (0, -6),
    (1, -3), (2, 1), (0, 2), (0, 7), (0, -4), (1, -1), (0, 4), (2, -1),
    (1, 2), (2, 3), (-1, -1), (-1, 2), (2, -2), (1, 5), (0, -7), (2, -3),
    (-1, 4), (1, -6), (1, -4), (2, -6), (0, 8), (0, 6), (-1, -6), (0, 5),
    (1, 7), (0, -5), (2, 7), (2, 4), (2, 2), (1, 4), (-1, 7), (1, 6),
    (2, 5), (2, -4), (-1, -4), (-1, 5), (1, -7), (2, -7), (-1, 8), (2, -5),
    (1, 8), (-1, -7), (-1, 6), (-1, -5), (1, -5), (2, 6), (2, 8),
)
TARGETS = {
    (-1, -6): ((-1, -7), (-1, -5)),
    (-1, -3): ((2, -3),),
    (-1, -2): ((2, -2),),
    (-1, 0): ((-1, 1),),
    (-1, 1): ((2, 1),),
    (-1, 3): ((-1, 4), (-1, 2)),
    (-1, 4): ((-1, 5),),
    (0, -7): ((1, -7),),
    (0, -6): ((2, -6), (-1, -6), (0, -7), (1, -6)),
    (0, -5): ((1, -5),),
    (0, -4): ((0, -5), (-1, -4)),
    (0, -3): ((-1, -3), (0, -4), (1, -3)),
    (0, -2): ((0, -6), (0, -1), (-1, -2), (1, -2)),
    (0, -1): ((2, -1), (-1, -1), (1, -1)),
    (0, 0): ((0, 3), (0, -2), (0, -3), (-1, 0), (0, 1), (2, 0), (1, 0)),
    (0, 1): ((1, 1),),
    (0, 3): ((0, 7), (1, 3), (-1, 3), (0, 4), (0, 2)),
    (0, 4): ((0, 5),),
    (0, 6): ((-1, 6),),
    (0, 7): ((2, 7), (0, 6), (0, 8), (-1, 7), (1, 7)),
    (0, 8): ((-1, 8), (1, 8)),
    (1, -3): ((1, -4),),
    (1, 2): ((2, 2),),
    (1, 3): ((1, 5), (1, 2), (2, 3)),
    (1, 5): ((1, 4), (1, 6), (2, 5)),
    (2, -6): ((2, -7), (2, -5)),
    (2, -3): ((2, -4),),
    (2, 3): ((2, 4),),
    (2, 7): ((2, 6), (2, 8)),
}
DEPARTURES = (
    (2, 6), (-1, 7), (2, 8), (-1, 8), (1, 8), (2, -7), (1, 7), (2, -6),
    (2, 4), (-1, -6), (1, 4), (1, 6), (2, -5), (2, -3), (1, -3), (2, -2),
    (2, 7), (-1, 6), (2, 2), (-1, -7), (0, 7), (0, 8), (0, -6), (1, -5),
    (1, -7), (1, 5), (1, -6), (-1, -5), (1, 2), (2, -4), (-1, 4), (0, 6),
    (2, 5), (2, 3), (-1, 5), (-1, -3), (0, -7), (-1, -2), (-1, 2), (1, -2),
    (2, 1), (-1, -4), (0, -5), (1, -4), (0, 2), (0, 4), (2, -1), (0, 5),
    (0, -3), (-1, 3), (1, 3), (-1, -1), (-1, 1), (0, -2), (1, -1), (1, 1),
    (2, 0), (0, -4), (0, 1), (0, 3), (-1, 0), (0, -1), (1, 0),
)
PARTS = {
    (2, 7): ((2, 6),),
    (-1, 6): ((-1, 7),),
    (-1, -7): ((-1, 8),),
    (0, 8): ((2, 8),),
    (1, -7): ((1, 8), (2, -7)),
    (1, 5): ((1, 7),),
    (1, -6): ((2, -6),),
    (-1, -5): ((-1, -6),),
    (2, -4): ((2, -5),),
    (-1, 4): ((1, 4),),
    (0, 6): ((1, 6),),
    (2, 5): ((2, 4), (2, 7)),
    (-1, 5): ((-1, 6),),
    (-1, -3): ((2, -3),),
    (0, -7): ((-1, -7), (0, 8), (1, -7)),
    (-1, 2): ((2, 2),),
    (1, -2): ((1, -3), (2, -2)),
    (-1, -4): ((2, -4),),
    (0, -5): ((0, -6), (-1, -5)),
    (1, -4): ((1, -5), (1, -6)),
    (0, 5): ((0, 7), (1, 5), (0, 6), (2, 5)),
    (0, -3): ((-1, -3),),
    (-1, 3): ((-1, 4), (-1, 5)),
    (1, 3): ((1, 2), (2, 3)),
    (-1, 1): ((-1, 2),),
    (0, -2): ((-1, -2), (1, -2)),
    (2, 0): ((2, 1),),
    (0, -4): ((0, -7), (-1, -4), (0, -5), (1, -4)),
    (0, 3): ((0, 2), (0, 4), (0, 5), (-1, 3), (1, 3)),
    (-1, 0): ((-1, 1),),
    (0, -1): ((2, -1), (0, -3), (-1, -1), (0, -2), (1, -1)),
    (1, 0): ((1, 1), (2, 0)),
    (0, 0): ((0, -4), (0, 1), (0, 3), (-1, 0), (0, -1), (1, 0)),
}
COPIES = len(ARRIVALS)
ARRIVAL = {node: i for i, node in enumerate(ARRIVALS)}
DEPARTURE = {node: i for i, node in enumerate(DEPARTURES)}
JOINS = {part: node for node, parts in PARTS.items() for part in parts}


def minus(a, b):
    dy, dz = (a[0] - b[0]) % NY, (a[1] - b[1]) % NZ
    return dy if dy <= NY // 2 else dy - NY, dz if dz <= NZ // 2 else dz - NZ


MOVES = sorted(
    {
        way
        for tree in (TARGETS, PARTS)
        for node, targets in tree.items()
        for target in targets
        for way in (minus(target, node), minus(node, target))
    }
)


def kernel(
    total_samples,
    x_hbm,
    u_hbm,
    o_ref,
    x_v,
    u_ref,
    gathered,
    score_slots,
    scatter_out,
    scatter_in,
    stat_z,
    stat_g,
    x_sem,
    u_sem,
    gather_send,
    gather_recv,
    score_send,
    score_recv,
    scatter_send,
    scatter_recv,
    stat_send,
    stat_recv,
):
    dp = lax.axis_index("dp")
    feat = lax.axis_index("feat")
    y = lax.div(dp, NZ)
    z = lax.rem(dp, NZ)

    way = 1 - 2 * lax.rem(feat, 2)

    def peer(dy, dz):
        return lax.rem(y + way * dy + NY, NY) * NZ + lax.rem(z + way * dz + NZ, NZ)

    def origin(node):
        return peer(-node[0], -node[1])

    def feat_peer(i):
        return lax.rem(feat + i, NF)

    x_copy = pltpu.make_async_copy(x_hbm, x_v, x_sem)
    u_copy = pltpu.make_async_copy(u_hbm, u_ref, u_sem)
    u_copy.start()
    x_copy.start()

    barrier = pltpu.get_barrier_semaphore()
    partners = [(peer(*move), feat) for move in MOVES]
    partners += [(dp, feat_peer(i)) for i in range(1, NF)]
    for partner in partners:
        pl.semaphore_signal(barrier, inc=1, device_id=partner, device_id_type=MESH)
    u_copy.wait()
    pl.semaphore_wait(barrier, len(partners))

    def gather_copy(node, target, src=None):
        index = origin(node)
        return pltpu.make_async_remote_copy(
            src_ref=gathered.at[index] if src is None else src,
            dst_ref=gathered.at[index],
            send_sem=gather_send,
            recv_sem=gather_recv.at[ARRIVAL[target]],
            device_id=(peer(*minus(target, node)), feat),
            device_id_type=MESH,
        )

    def arrived(node):
        shard = gathered.at[origin(node)]
        pltpu.make_async_copy(shard, shard, gather_recv.at[ARRIVAL[node]]).wait()

    for target in TARGETS[ROOT]:
        gather_copy(ROOT, target, u_ref).start()
    gathered[dp] = u_ref[...]

    def columns_of(index):
        return pl.ds(pl.multiple_of(index * WIDTH, WIDTH), WIDTH)

    def partial_scores(acc, nodes):
        for node in nodes:
            index = origin(node)
            acc = acc + lax.dot_general(
                gathered[index],
                x_v[:, columns_of(index)],
                (((1,), (1,)), ((), ())),
                preferred_element_type=jnp.float32,
            )
        return acc

    x_copy.wait()
    acc = partial_scores(jnp.zeros((K, ROWS), jnp.float32), (ROOT,))
    for start in range(0, COPIES, GROUP):
        group = ARRIVALS[start : start + GROUP]
        for node in group:
            arrived(node)
            for target in TARGETS.get(node, ()):
                gather_copy(node, target).start()
        acc = partial_scores(acc, group)

    score_slots[feat] = acc.astype(jnp.bfloat16)

    def score_copy(i):
        return pltpu.make_async_remote_copy(
            src_ref=score_slots.at[feat],
            dst_ref=score_slots.at[feat],
            send_sem=score_send,
            recv_sem=score_recv,
            device_id=(dp, feat_peer(i)),
            device_id_type=MESH,
        )

    for i in range(1, NF):
        score_copy(i).start()
    seven = score_slots.at[pl.ds(0, NF - 1)]
    pltpu.make_async_copy(seven, seven, score_recv).wait()
    summed = score_slots[0].astype(jnp.float32)
    for i in range(1, NF):
        summed = summed + score_slots[i].astype(jnp.float32)
    scores = (summed * (1.0 / math.sqrt(F))).astype(jnp.bfloat16)

    gram = lax.dot_general(
        scores, scores, (((1,), (1,)), ((), ())), preferred_element_type=jnp.float32
    )
    below = lax.broadcasted_iota(jnp.int32, (K, K), 0) > lax.broadcasted_iota(
        jnp.int32, (K, K), 1
    )
    penalty = jnp.where(below, gram * (-1.0 / math.sqrt(F)), 0.0)
    high = penalty.astype(jnp.bfloat16)
    low = (penalty - high.astype(jnp.float32)).astype(jnp.bfloat16)
    weights = jnp.concatenate([scores, high, low], axis=1)

    def term(node):
        index = origin(node)
        shard = gathered[index]
        return jnp.dot(
            weights,
            jnp.concatenate([x_v[:, columns_of(index)], shard, shard], axis=0),
            preferred_element_type=jnp.float32,
        )

    def scatter_copy(node):
        slot = DEPARTURE[node]
        return pltpu.make_async_remote_copy(
            src_ref=scatter_out.at[slot],
            dst_ref=scatter_in.at[slot],
            send_sem=scatter_send,
            recv_sem=scatter_recv.at[slot],
            device_id=(peer(*minus(JOINS[node], node)), feat),
            device_id_type=MESH,
        )

    def take(total, node):
        for part in PARTS.get(node, ()):
            slot = DEPARTURE[part]
            pltpu.make_async_copy(
                scatter_in.at[slot], scatter_in.at[slot], scatter_recv.at[slot]
            ).wait()
            total = total + scatter_in[slot].astype(jnp.float32)
        return total

    stops = DEPARTURES + (ROOT,)
    terms = [term(node) for node in stops[:AHEAD]]
    for i, node in enumerate(stops):
        if i + AHEAD < len(stops):
            terms.append(term(stops[i + AHEAD]))
        total = take(terms.pop(0), node)
        if node != ROOT:
            scatter_out[DEPARTURE[node]] = total.astype(jnp.bfloat16)
            scatter_copy(node).start()
    own = total

    current = u_ref[...].astype(jnp.float32)
    update = own * (math.sqrt(F) / total_samples)
    lane_of = lax.broadcasted_iota(jnp.int32, (K, 128), 1)
    stats = jnp.zeros((K, 128), jnp.float32)
    for lane, value in enumerate((current * current, current * update, update * update)):
        column = jnp.sum(value, axis=1, keepdims=True)
        stats = jnp.where(lane_of == lane, column, stats)
    stats = jnp.concatenate([stats, jnp.zeros_like(stats)], axis=0).T[:8]

    def ring(i, count):
        return min(i, count - i)

    def total_over(stage, slots, me, count, device_of, distance, value):
        slots[me] = value
        for i in sorted(range(1, count), key=distance, reverse=True):
            pltpu.make_async_remote_copy(
                src_ref=slots.at[me],
                dst_ref=slots.at[me],
                send_sem=stat_send.at[stage],
                recv_sem=stat_recv.at[stage],
                device_id=device_of(i),
                device_id_type=MESH,
            ).start()
        others = slots.at[pl.ds(0, count - 1)]
        pltpu.make_async_copy(others, others, stat_recv.at[stage]).wait()
        total = slots[0]
        for i in range(1, count):
            total = total + slots[i]
        return total

    def group(i):
        return (peer(i // NF, 0), feat_peer(i % NF))

    def group_distance(i):
        return 2 * ring(i // NF, NY) + ring(i % NF, NF)

    stats = total_over(1, stat_g, y * NF + feat, NY * NF, group, group_distance, stats)
    stats = total_over(0, stat_z, z, NZ, lambda i: (peer(0, i), feat), lambda i: ring(i, NZ), stats)

    columns = jnp.concatenate([stats, jnp.zeros((120, 128), jnp.float32)], axis=0).T[:K]
    columns = columns * (1.0 / F)
    alignment = columns[:, 1:2]
    keep = 1.0 - STEP * alignment
    squares = (
        keep * keep * columns[:, 0:1]
        + 2.0 * STEP * keep * alignment
        + STEP * STEP * columns[:, 2:3]
    )
    scale = lax.rsqrt(jnp.maximum(squares, 0.0) + EPSILON)
    o_ref[...] = ((keep * current + STEP * update) * scale).astype(jnp.bfloat16)

    sent = gathered.at[pl.ds(0, COPIES)]
    pltpu.make_async_copy(sent, sent, gather_send).wait()
    pltpu.make_async_copy(seven, seven, score_send).wait()
    pltpu.make_async_copy(sent, sent, scatter_send).wait()
    for stage, (slots, count) in enumerate(((stat_z, NZ), (stat_g, NY * NF))):
        others = slots.at[pl.ds(0, count - 1)]
        pltpu.make_async_copy(others, others, stat_send.at[stage]).wait()


def shards(samples, estimates):
    shaped = estimates.reshape(K, WIDTH)
    total_samples = samples.shape[0] * lax.axis_size("dp")
    bf16, f32 = jnp.bfloat16, jnp.float32
    dma = pltpu.SemaphoreType.DMA
    updated = pl.pallas_call(
        functools.partial(kernel, total_samples),
        out_shape=jax.ShapeDtypeStruct((K, WIDTH), bf16),
        in_specs=[
            pl.BlockSpec(memory_space=pl.ANY),
            pl.BlockSpec(memory_space=pl.ANY),
        ],
        out_specs=pl.BlockSpec(memory_space=pltpu.VMEM),
        scratch_shapes=[
            pltpu.VMEM((ROWS, NY * NZ * WIDTH), bf16),
            pltpu.VMEM((K, WIDTH), bf16),
            pltpu.VMEM((NY * NZ, K, WIDTH), bf16),
            pltpu.VMEM((NF, K, ROWS), bf16),
            pltpu.VMEM((COPIES, K, WIDTH), bf16),
            pltpu.VMEM((COPIES, K, WIDTH), bf16),
            pltpu.VMEM((NZ, 8, 128), f32),
            pltpu.VMEM((NY * NF, 8, 128), f32),
            dma,
            dma,
            dma,
            dma((COPIES,)),
            dma,
            dma,
            dma,
            dma((COPIES,)),
            dma((2,)),
            dma((2,)),
        ],
        compiler_params=pltpu.CompilerParams(
            collective_id=0,
            has_side_effects=True,
            vmem_limit_bytes=60 * 1024 * 1024,
        ),
        cost_estimate=pl.CostEstimate(
            flops=4 * K * ROWS * NY * NZ * WIDTH,
            bytes_accessed=2 * ROWS * NY * NZ * WIDTH,
            transcendentals=0,
        ),
    )(samples, shaped)
    return updated.reshape(K, 1, WIDTH)


def solution(mesh):
    return jax.shard_map(
        shards,
        mesh=mesh,
        in_specs=(P("dp", "feat"), P(None, "feat", "dp")),
        out_specs=P(None, "feat", "dp"),
        check_vma=False,
    )
```

```python
import functools
import math

import jax
import jax.numpy as jnp
from jax import lax
from jax.experimental import pallas as pl
from jax.experimental.pallas import tpu as pltpu
from jax.sharding import PartitionSpec as P

F = 131072
STEP = 0.05
EPSILON = 1e-06
MESH = pl.DeviceIdType.MESH
GROUP = 2
AHEAD = 3
ROOT = (0, 0)

NY, NZ, NF = 4, 16, 8
K = 64
ROWS = 128
WIDTH = 256

ARRIVALS = (
    (-1, 0), (0, -2), (1, 0), (2, 0), (0, 3), (0, 1), (0, -3), (-1, 1),
    (0, -1), (-1, -2), (1, -2), (1, 3), (-1, 3), (1, 1), (-1, -3), (0, -6),
    (1, -3), (2, 1), (0, 2), (0, 7), (0, -4), (1, -1), (0, 4), (2, -1),
    (1, 2), (2, 3), (-1, -1), (-1, 2), (2, -2), (1, 5), (0, -7), (2, -3),
    (-1, 4), (1, -6), (1, -4), (2, -6), (0, 8), (0, 6), (-1, -6), (0, 5),
    (1, 7), (0, -5), (2, 7), (2, 4), (2, 2), (1, 4), (-1, 7), (1, 6),
    (2, 5), (2, -4), (-1, -4), (-1, 5), (1, -7), (2, -7), (-1, 8), (2, -5),
    (1, 8), (-1, -7), (-1, 6), (-1, -5), (1, -5), (2, 6), (2, 8),
)
TARGETS = {
    (-1, -6): ((-1, -7), (-1, -5)),
    (-1, -3): ((2, -3),),
    (-1, -2): ((2, -2),),
    (-1, 0): ((-1, 1),),
    (-1, 1): ((2, 1),),
    (-1, 3): ((-1, 4), (-1, 2)),
    (-1, 4): ((-1, 5),),
    (0, -7): ((1, -7),),
    (0, -6): ((2, -6), (-1, -6), (0, -7), (1, -6)),
    (0, -5): ((1, -5),),
    (0, -4): ((0, -5), (-1, -4)),
    (0, -3): ((-1, -3), (0, -4), (1, -3)),
    (0, -2): ((0, -6), (0, -1), (-1, -2), (1, -2)),
    (0, -1): ((2, -1), (-1, -1), (1, -1)),
    (0, 0): ((0, 3), (0, -2), (0, -3), (-1, 0), (0, 1), (2, 0), (1, 0)),
    (0, 1): ((1, 1),),
    (0, 3): ((0, 7), (1, 3), (-1, 3), (0, 4), (0, 2)),
    (0, 4): ((0, 5),),
    (0, 6): ((-1, 6),),
    (0, 7): ((2, 7), (0, 6), (0, 8), (-1, 7), (1, 7)),
    (0, 8): ((-1, 8), (1, 8)),
    (1, -3): ((1, -4),),
    (1, 2): ((2, 2),),
    (1, 3): ((1, 5), (1, 2), (2, 3)),
    (1, 5): ((1, 4), (1, 6), (2, 5)),
    (2, -6): ((2, -7), (2, -5)),
    (2, -3): ((2, -4),),
    (2, 3): ((2, 4),),
    (2, 7): ((2, 6), (2, 8)),
}
DEPARTURES = (
    (2, 8), (2, 7), (0, -3), (0, 1), (2, -3), (1, 8), (2, -7), (-1, -7),
    (-1, 7), (1, -7), (1, 7), (-1, -6), (-1, 4), (1, 2), (1, 6), (2, -5),
    (2, 3), (2, 5), (-1, 3), (0, -2), (2, -2), (2, 2), (1, -5), (1, -3),
    (2, -4), (1, -2), (-1, 8), (2, 6), (0, 2), (-1, -3), (2, -6), (0, -7),
    (1, -6), (0, 7), (-1, -5), (-1, 5), (1, 3), (0, -5), (1, 5), (2, 4),
    (0, 8), (0, -1), (-1, 6), (2, -1), (-1, 2), (2, 1), (1, -4), (1, -1),
    (-1, -2), (0, -6), (-1, -4), (0, 3), (0, 5), (1, 4), (0, 6), (2, 0),
    (1, 1), (-1, 1), (-1, -1), (0, -4), (0, 4), (1, 0), (-1, 0),
)
PARTS = {
    (-1, 8): ((2, 8),),
    (2, 6): ((2, 7),),
    (0, 2): ((0, 1),),
    (-1, -3): ((0, -3), (2, -3)),
    (2, -6): ((2, -7),),
    (0, -7): ((-1, -7),),
    (1, -6): ((1, -7),),
    (0, 7): ((1, 7),),
    (-1, -5): ((-1, -6), (2, -5)),
    (-1, 5): ((-1, 4),),
    (1, 3): ((1, 2),),
    (0, -5): ((1, -5),),
    (1, 5): ((1, 6), (2, 5)),
    (2, 4): ((2, 3),),
    (0, 8): ((1, 8), (-1, 8)),
    (0, -1): ((0, -2),),
    (-1, 6): ((-1, 7), (2, 6)),
    (2, -1): ((2, -2),),
    (-1, 2): ((-1, 3), (0, 2)),
    (2, 1): ((2, 2),),
    (1, -4): ((1, -3), (2, -4)),
    (1, -1): ((1, -2),),
    (-1, -2): ((-1, -3),),
    (0, -6): ((2, -6), (0, -7), (1, -6)),
    (-1, -4): ((-1, -5),),
    (0, 3): ((1, 3),),
    (0, 5): ((-1, 5), (1, 5)),
    (1, 4): ((2, 4),),
    (0, 6): ((0, 7), (0, 8), (-1, 6)),
    (2, 0): ((2, -1),),
    (1, 1): ((2, 1),),
    (-1, 1): ((-1, 2),),
    (-1, -1): ((0, -1), (-1, -2)),
    (0, -4): ((0, -5), (1, -4), (0, -6), (-1, -4)),
    (0, 4): ((0, 3), (0, 5), (1, 4), (0, 6)),
    (1, 0): ((1, -1), (2, 0), (1, 1)),
    (-1, 0): ((-1, 1), (-1, -1)),
    (0, 0): ((0, -4), (0, 4), (1, 0), (-1, 0)),
}
COPIES = len(ARRIVALS)
ARRIVAL = {node: i for i, node in enumerate(ARRIVALS)}
DEPARTURE = {node: i for i, node in enumerate(DEPARTURES)}
JOINS = {part: node for node, parts in PARTS.items() for part in parts}


def minus(a, b):
    dy, dz = (a[0] - b[0]) % NY, (a[1] - b[1]) % NZ
    return dy if dy <= NY // 2 else dy - NY, dz if dz <= NZ // 2 else dz - NZ


MOVES = sorted(
    {
        way
        for tree in (TARGETS, PARTS)
        for node, targets in tree.items()
        for target in targets
        for way in (minus(target, node), minus(node, target))
    }
)


def kernel(
    total_samples,
    x_hbm,
    u_hbm,
    o_ref,
    x_v,
    u_ref,
    gathered,
    score_slots,
    scatter_out,
    scatter_in,
    stat_z,
    stat_g,
    x_sem,
    u_sem,
    gather_send,
    gather_recv,
    score_send,
    score_recv,
    scatter_send,
    scatter_recv,
    stat_send,
    stat_recv,
):
    dp = lax.axis_index("dp")
    feat = lax.axis_index("feat")
    y = lax.div(dp, NZ)
    z = lax.rem(dp, NZ)

    way = 1 - 2 * lax.rem(feat, 2)

    def peer(dy, dz, way=way):
        return lax.rem(y + way * dy + NY, NY) * NZ + lax.rem(z + way * dz + NZ, NZ)

    def origin(node, way=way):
        return peer(-node[0], -node[1], way)

    def feat_peer(i):
        return lax.rem(feat + i, NF)

    x_copy = pltpu.make_async_copy(x_hbm, x_v, x_sem)
    u_copy = pltpu.make_async_copy(u_hbm, u_ref, u_sem)
    u_copy.start()
    x_copy.start()

    barrier = pltpu.get_barrier_semaphore()
    partners = [(peer(*move), feat) for move in MOVES]
    partners += [(dp, feat_peer(i)) for i in range(1, NF)]
    for partner in partners:
        pl.semaphore_signal(barrier, inc=1, device_id=partner, device_id_type=MESH)
    u_copy.wait()
    pl.semaphore_wait(barrier, len(partners))

    def gather_copy(node, target, src=None):
        index = origin(node, 1)
        return pltpu.make_async_remote_copy(
            src_ref=gathered.at[index] if src is None else src,
            dst_ref=gathered.at[index],
            send_sem=gather_send,
            recv_sem=gather_recv.at[ARRIVAL[target]],
            device_id=(peer(*minus(target, node), 1), feat),
            device_id_type=MESH,
        )

    def arrived(node):
        shard = gathered.at[origin(node, 1)]
        pltpu.make_async_copy(shard, shard, gather_recv.at[ARRIVAL[node]]).wait()

    for target in TARGETS[ROOT]:
        gather_copy(ROOT, target, u_ref).start()
    gathered[dp] = u_ref[...]

    def columns_of(index):
        return pl.ds(pl.multiple_of(index * WIDTH, WIDTH), WIDTH)

    def partial_scores(acc, nodes):
        for node in nodes:
            index = origin(node, 1)
            acc = acc + lax.dot_general(
                gathered[index],
                x_v[:, columns_of(index)],
                (((1,), (1,)), ((), ())),
                preferred_element_type=jnp.float32,
            )
        return acc

    x_copy.wait()
    acc = partial_scores(jnp.zeros((K, ROWS), jnp.float32), (ROOT,))
    for start in range(0, COPIES, GROUP):
        group = ARRIVALS[start : start + GROUP]
        for node in group:
            arrived(node)
            for target in TARGETS.get(node, ()):
                gather_copy(node, target).start()
        acc = partial_scores(acc, group)

    score_slots[feat] = acc.astype(jnp.bfloat16)

    def score_copy(i):
        return pltpu.make_async_remote_copy(
            src_ref=score_slots.at[feat],
            dst_ref=score_slots.at[feat],
            send_sem=score_send,
            recv_sem=score_recv,
            device_id=(dp, feat_peer(i)),
            device_id_type=MESH,
        )

    for i in range(1, NF):
        score_copy(i).start()
    seven = score_slots.at[pl.ds(0, NF - 1)]
    pltpu.make_async_copy(seven, seven, score_recv).wait()
    summed = score_slots[0].astype(jnp.float32)
    for i in range(1, NF):
        summed = summed + score_slots[i].astype(jnp.float32)
    scores = (summed * (1.0 / math.sqrt(F))).astype(jnp.bfloat16)

    gram = lax.dot_general(
        scores, scores, (((1,), (1,)), ((), ())), preferred_element_type=jnp.float32
    )
    below = lax.broadcasted_iota(jnp.int32, (K, K), 0) > lax.broadcasted_iota(
        jnp.int32, (K, K), 1
    )
    penalty = jnp.where(below, gram * (-1.0 / math.sqrt(F)), 0.0)
    high = penalty.astype(jnp.bfloat16)
    low = (penalty - high.astype(jnp.float32)).astype(jnp.bfloat16)
    weights = jnp.concatenate([scores, high, low], axis=1)

    def term(node):
        index = origin(node)
        shard = gathered[index]
        return jnp.dot(
            weights,
            jnp.concatenate([x_v[:, columns_of(index)], shard, shard], axis=0),
            preferred_element_type=jnp.float32,
        )

    def scatter_copy(node):
        slot = DEPARTURE[node]
        return pltpu.make_async_remote_copy(
            src_ref=scatter_out.at[slot],
            dst_ref=scatter_in.at[slot],
            send_sem=scatter_send,
            recv_sem=scatter_recv.at[slot],
            device_id=(peer(*minus(JOINS[node], node)), feat),
            device_id_type=MESH,
        )

    def take(total, node):
        for part in PARTS.get(node, ()):
            slot = DEPARTURE[part]
            pltpu.make_async_copy(
                scatter_in.at[slot], scatter_in.at[slot], scatter_recv.at[slot]
            ).wait()
            total = total + scatter_in[slot].astype(jnp.float32)
        return total

    stops = DEPARTURES + (ROOT,)
    terms = [term(node) for node in stops[:AHEAD]]
    for i, node in enumerate(stops):
        if i + AHEAD < len(stops):
            terms.append(term(stops[i + AHEAD]))
        total = take(terms.pop(0), node)
        if node != ROOT:
            scatter_out[DEPARTURE[node]] = total.astype(jnp.bfloat16)
            scatter_copy(node).start()
    own = total

    current = u_ref[...].astype(jnp.float32)
    update = own * (math.sqrt(F) / total_samples)
    lane_of = lax.broadcasted_iota(jnp.int32, (K, 128), 1)

    def row_sum(value):
        return jnp.sum(value, axis=1, keepdims=True)

    stats = jnp.concatenate(
        [
            jnp.where(
                lane_of == 0,
                row_sum(current * current),
                jnp.where(lane_of == 1, row_sum(update * update), 0.0),
            ),
            jnp.where(lane_of == 0, row_sum(current * update), 0.0),
        ],
        axis=0,
    ).T[:2]

    def ring(i, count):
        return min(i, count - i)

    def total_over(stage, slots, me, count, device_of, distance, value):
        slots[me] = value
        for i in sorted(range(1, count), key=distance, reverse=True):
            pltpu.make_async_remote_copy(
                src_ref=slots.at[me],
                dst_ref=slots.at[me],
                send_sem=stat_send.at[stage],
                recv_sem=stat_recv.at[stage],
                device_id=device_of(i),
                device_id_type=MESH,
            ).start()
        others = slots.at[pl.ds(0, count - 1)]
        pltpu.make_async_copy(others, others, stat_recv.at[stage]).wait()
        total = slots[0]
        for i in range(1, count):
            total = total + slots[i]
        return total

    def group(i):
        return (peer(i // NF, 0), feat_peer(i % NF))

    def group_distance(i):
        return 2 * ring(i // NF, NY) + ring(i % NF, NF)

    stats = total_over(1, stat_g, y * NF + feat, NY * NF, group, group_distance, stats)
    stats = total_over(0, stat_z, z, NZ, lambda i: (peer(0, i), feat), lambda i: ring(i, NZ), stats)

    row_of = lax.broadcasted_iota(jnp.int32, (8, 128), 0)
    rows = jnp.where(row_of == 0, stats[0:1], jnp.where(row_of == 1, stats[1:2], 0.0))
    columns = jnp.concatenate([rows, jnp.zeros((120, 128), jnp.float32)], axis=0).T
    columns = columns * (1.0 / F)
    alignment = columns[K:, 0:1]
    keep = 1.0 - STEP * alignment
    squares = (
        keep * keep * columns[:K, 0:1]
        + 2.0 * STEP * keep * alignment
        + STEP * STEP * columns[:K, 1:2]
    )
    scale = lax.rsqrt(jnp.maximum(squares, 0.0) + EPSILON)
    o_ref[...] = ((keep * current + STEP * update) * scale).astype(jnp.bfloat16)

    sent = gathered.at[pl.ds(0, COPIES)]
    pltpu.make_async_copy(sent, sent, gather_send).wait()
    pltpu.make_async_copy(seven, seven, score_send).wait()
    pltpu.make_async_copy(sent, sent, scatter_send).wait()
    for stage, (slots, count) in enumerate(((stat_z, NZ), (stat_g, NY * NF))):
        others = slots.at[pl.ds(0, count - 1)]
        pltpu.make_async_copy(others, others, stat_send.at[stage]).wait()


def shards(samples, estimates):
    shaped = estimates.reshape(K, WIDTH)
    total_samples = samples.shape[0] * lax.axis_size("dp")
    bf16, f32 = jnp.bfloat16, jnp.float32
    dma = pltpu.SemaphoreType.DMA
    updated = pl.pallas_call(
        functools.partial(kernel, total_samples),
        out_shape=jax.ShapeDtypeStruct((K, WIDTH), bf16),
        in_specs=[
            pl.BlockSpec(memory_space=pl.ANY),
            pl.BlockSpec(memory_space=pl.ANY),
        ],
        out_specs=pl.BlockSpec(memory_space=pltpu.VMEM),
        scratch_shapes=[
            pltpu.VMEM((ROWS, NY * NZ * WIDTH), bf16),
            pltpu.VMEM((K, WIDTH), bf16),
            pltpu.VMEM((NY * NZ, K, WIDTH), bf16),
            pltpu.VMEM((NF, K, ROWS), bf16),
            pltpu.VMEM((COPIES, K, WIDTH), bf16),
            pltpu.VMEM((COPIES, K, WIDTH), bf16),
            pltpu.VMEM((NZ, 2, 128), f32),
            pltpu.VMEM((NY * NF, 2, 128), f32),
            dma,
            dma,
            dma,
            dma((COPIES,)),
            dma,
            dma,
            dma,
            dma((COPIES,)),
            dma((2,)),
            dma((2,)),
        ],
        compiler_params=pltpu.CompilerParams(
            collective_id=0,
            has_side_effects=True,
            vmem_limit_bytes=60 * 1024 * 1024,
        ),
        cost_estimate=pl.CostEstimate(
            flops=4 * K * ROWS * NY * NZ * WIDTH,
            bytes_accessed=2 * ROWS * NY * NZ * WIDTH,
            transcendentals=0,
        ),
    )(samples, shaped)
    return updated.reshape(K, 1, WIDTH)


def solution(mesh):
    return jax.shard_map(
        shards,
        mesh=mesh,
        in_specs=(P("dp", "feat"), P(None, "feat", "dp")),
        out_specs=P(None, "feat", "dp"),
        check_vma=False,
    )
```

```python
import functools
import math

import jax
import jax.numpy as jnp
from jax import lax
from jax.experimental import pallas as pl
from jax.experimental.pallas import tpu as pltpu
from jax.sharding import PartitionSpec as P

F = 131072
STEP = 0.05
EPSILON = 1e-06
MESH = pl.DeviceIdType.MESH
GROUP = 2
AHEAD = 3
ROOT = (0, 0)

NY, NZ, NF = 4, 16, 8
K = 64
ROWS = 128
WIDTH = 256

ARRIVALS = (
    (-1, 0), (1, 0), (2, 0), (0, 4), (0, -4), (0, 1), (-1, -2), (-1, -1),
    (2, 2), (2, -1), (-1, 4), (1, 4), (0, 3), (-1, -4), (1, -4), (-1, 1),
    (1, 1), (0, 7), (0, -6), (2, -2), (0, -2), (0, 5), (0, -5), (1, 2),
    (-1, 2), (0, 2), (-1, -3), (1, -1), (2, 4), (-1, 5), (1, 3), (-1, 3),
    (2, -4), (1, 5), (2, 1), (1, -3), (1, 7), (2, 7), (0, 8), (1, -6),
    (-1, -7), (-1, 7), (0, 6), (1, -2), (-1, -6), (-1, -5), (-1, 6), (2, 3),
    (0, -7), (0, -1), (1, 6), (2, 5), (0, -3), (2, -5), (1, 8), (2, -3),
    (2, 6), (-1, 8), (2, 8), (2, -6), (1, -7), (2, -7), (1, -5),
)
TARGETS = {
    (-1, -7): ((2, -7),),
    (-1, -4): ((-1, -7), (-1, -5)),
    (-1, -2): ((0, -2), (-1, -3), (2, -2)),
    (-1, 0): ((-1, -2), (-1, -1)),
    (-1, 1): ((2, 1),),
    (-1, 4): ((-1, 5),),
    (-1, 5): ((-1, 6),),
    (0, -6): ((1, -6), (-1, -6), (0, -7)),
    (0, -4): ((-1, -4), (0, -6), (1, -4), (0, -5)),
    (0, -2): ((1, -2),),
    (0, 0): ((0, 4), (0, -4), (-1, 0), (2, 0), (0, 1), (1, 0)),
    (0, 1): ((-1, 1), (0, 2), (1, 1)),
    (0, 3): ((-1, 3),),
    (0, 4): ((0, 7), (-1, 4), (1, 4), (0, 3), (0, 5)),
    (0, 5): ((0, 6),),
    (0, 7): ((2, 7), (0, 8), (1, 7), (-1, 7)),
    (0, 8): ((-1, 8),),
    (1, -6): ((1, -7), (1, -5), (2, -6)),
    (1, -4): ((1, -3), (2, -4)),
    (1, -3): ((0, -3), (2, -3)),
    (1, -1): ((0, -1),),
    (1, 3): ((2, 3),),
    (1, 4): ((1, 3), (1, 5), (2, 4)),
    (1, 5): ((1, 6), (2, 5)),
    (1, 7): ((1, 8),),
    (2, -4): ((2, -5),),
    (2, -1): ((1, -1),),
    (2, 0): ((2, -1), (2, 2)),
    (2, 2): ((-1, 2), (1, 2)),
    (2, 7): ((2, 6), (2, 8)),
}
DEPARTURES = (
    (2, 8), (2, 7), (0, -3), (0, 1), (2, -3), (1, 8), (2, -7), (-1, -7),
    (-1, 7), (1, -7), (1, 7), (-1, -6), (-1, 4), (1, 2), (1, 6), (2, -5),
    (2, 3), (2, 5), (-1, 3), (0, -2), (2, -2), (2, 2), (1, -5), (1, -3),
    (2, -4), (1, -2), (-1, 8), (2, 6), (0, 2), (-1, -3), (2, -6), (0, -7),
    (1, -6), (0, 7), (-1, -5), (-1, 5), (1, 3), (0, -5), (1, 5), (2, 4),
    (0, 8), (0, -1), (-1, 6), (2, -1), (-1, 2), (2, 1), (1, -4), (1, -1),
    (-1, -2), (0, -6), (-1, -4), (0, 3), (0, 5), (1, 4), (0, 6), (2, 0),
    (1, 1), (-1, 1), (-1, -1), (0, -4), (0, 4), (1, 0), (-1, 0),
)
PARTS = {
    (-1, 8): ((2, 8),),
    (2, 6): ((2, 7),),
    (0, 2): ((0, 1),),
    (-1, -3): ((0, -3), (2, -3)),
    (2, -6): ((2, -7),),
    (0, -7): ((-1, -7),),
    (1, -6): ((1, -7),),
    (0, 7): ((1, 7),),
    (-1, -5): ((-1, -6), (2, -5)),
    (-1, 5): ((-1, 4),),
    (1, 3): ((1, 2),),
    (0, -5): ((1, -5),),
    (1, 5): ((1, 6), (2, 5)),
    (2, 4): ((2, 3),),
    (0, 8): ((1, 8), (-1, 8)),
    (0, -1): ((0, -2),),
    (-1, 6): ((-1, 7), (2, 6)),
    (2, -1): ((2, -2),),
    (-1, 2): ((-1, 3), (0, 2)),
    (2, 1): ((2, 2),),
    (1, -4): ((1, -3), (2, -4)),
    (1, -1): ((1, -2),),
    (-1, -2): ((-1, -3),),
    (0, -6): ((2, -6), (0, -7), (1, -6)),
    (-1, -4): ((-1, -5),),
    (0, 3): ((1, 3),),
    (0, 5): ((-1, 5), (1, 5)),
    (1, 4): ((2, 4),),
    (0, 6): ((0, 7), (0, 8), (-1, 6)),
    (2, 0): ((2, -1),),
    (1, 1): ((2, 1),),
    (-1, 1): ((-1, 2),),
    (-1, -1): ((0, -1), (-1, -2)),
    (0, -4): ((0, -5), (1, -4), (0, -6), (-1, -4)),
    (0, 4): ((0, 3), (0, 5), (1, 4), (0, 6)),
    (1, 0): ((1, -1), (2, 0), (1, 1)),
    (-1, 0): ((-1, 1), (-1, -1)),
    (0, 0): ((0, -4), (0, 4), (1, 0), (-1, 0)),
}
COPIES = len(ARRIVALS)
ARRIVAL = {node: i for i, node in enumerate(ARRIVALS)}
DEPARTURE = {node: i for i, node in enumerate(DEPARTURES)}
JOINS = {part: node for node, parts in PARTS.items() for part in parts}


def minus(a, b):
    dy, dz = (a[0] - b[0]) % NY, (a[1] - b[1]) % NZ
    return dy if dy <= NY // 2 else dy - NY, dz if dz <= NZ // 2 else dz - NZ


MOVES = sorted(
    {
        way
        for tree in (TARGETS, PARTS)
        for node, targets in tree.items()
        for target in targets
        for way in (minus(target, node), minus(node, target))
    }
)


def kernel(
    total_samples,
    x_hbm,
    u_hbm,
    o_ref,
    x_v,
    u_ref,
    gathered,
    score_slots,
    scatter_out,
    scatter_in,
    stat_z,
    stat_g,
    x_sem,
    u_sem,
    gather_send,
    gather_recv,
    score_send,
    score_recv,
    scatter_send,
    scatter_recv,
    stat_send,
    stat_recv,
):
    dp = lax.axis_index("dp")
    feat = lax.axis_index("feat")
    y = lax.div(dp, NZ)
    z = lax.rem(dp, NZ)

    way = 1 - 2 * lax.rem(feat, 2)

    def peer(dy, dz, way=way):
        return lax.rem(y + way * dy + NY, NY) * NZ + lax.rem(z + way * dz + NZ, NZ)

    def origin(node, way=way):
        return peer(-node[0], -node[1], way)

    def feat_peer(i):
        return lax.rem(feat + i, NF)

    x_copy = pltpu.make_async_copy(x_hbm, x_v, x_sem)
    u_copy = pltpu.make_async_copy(u_hbm, u_ref, u_sem)
    u_copy.start()
    x_copy.start()

    barrier = pltpu.get_barrier_semaphore()
    partners = [(peer(*move), feat) for move in MOVES]
    partners += [(dp, feat_peer(i)) for i in range(1, NF)]
    for partner in partners:
        pl.semaphore_signal(barrier, inc=1, device_id=partner, device_id_type=MESH)
    u_copy.wait()
    pl.semaphore_wait(barrier, len(partners))

    def gather_copy(node, target, src=None):
        index = origin(node, 1)
        return pltpu.make_async_remote_copy(
            src_ref=gathered.at[index] if src is None else src,
            dst_ref=gathered.at[index],
            send_sem=gather_send,
            recv_sem=gather_recv.at[ARRIVAL[target]],
            device_id=(peer(*minus(target, node), 1), feat),
            device_id_type=MESH,
        )

    def arrived(node):
        shard = gathered.at[origin(node, 1)]
        pltpu.make_async_copy(shard, shard, gather_recv.at[ARRIVAL[node]]).wait()

    for target in TARGETS[ROOT]:
        gather_copy(ROOT, target, u_ref).start()
    gathered[dp] = u_ref[...]

    def columns_of(index):
        return pl.ds(pl.multiple_of(index * WIDTH, WIDTH), WIDTH)

    def partial_scores(acc, nodes):
        for node in nodes:
            index = origin(node, 1)
            acc = acc + lax.dot_general(
                gathered[index],
                x_v[:, columns_of(index)],
                (((1,), (1,)), ((), ())),
                preferred_element_type=jnp.float32,
            )
        return acc

    x_copy.wait()
    acc = partial_scores(jnp.zeros((K, ROWS), jnp.float32), (ROOT,))
    for start in range(0, COPIES, GROUP):
        group = ARRIVALS[start : start + GROUP]
        for node in group:
            arrived(node)
            for target in TARGETS.get(node, ()):
                gather_copy(node, target).start()
        acc = partial_scores(acc, group)

    score_slots[feat] = acc.astype(jnp.bfloat16)

    def score_copy(i):
        return pltpu.make_async_remote_copy(
            src_ref=score_slots.at[feat],
            dst_ref=score_slots.at[feat],
            send_sem=score_send,
            recv_sem=score_recv,
            device_id=(dp, feat_peer(i)),
            device_id_type=MESH,
        )

    for i in (4, 3, 5, 2, 6, 1, 7):
        score_copy(i).start()
    seven = score_slots.at[pl.ds(0, NF - 1)]
    pltpu.make_async_copy(seven, seven, score_recv).wait()
    summed = score_slots[0].astype(jnp.float32)
    for i in range(1, NF):
        summed = summed + score_slots[i].astype(jnp.float32)
    scores = (summed * (1.0 / math.sqrt(F))).astype(jnp.bfloat16)

    gram = lax.dot_general(
        scores, scores, (((1,), (1,)), ((), ())), preferred_element_type=jnp.float32
    )
    below = lax.broadcasted_iota(jnp.int32, (K, K), 0) > lax.broadcasted_iota(
        jnp.int32, (K, K), 1
    )
    penalty = jnp.where(below, gram * (-1.0 / math.sqrt(F)), 0.0)
    high = penalty.astype(jnp.bfloat16)
    low = (penalty - high.astype(jnp.float32)).astype(jnp.bfloat16)
    weights = jnp.concatenate([scores, high, low], axis=1)

    def term(node):
        index = origin(node)
        shard = gathered[index]
        return jnp.dot(
            weights,
            jnp.concatenate([x_v[:, columns_of(index)], shard, shard], axis=0),
            preferred_element_type=jnp.float32,
        )

    def scatter_copy(node):
        slot = DEPARTURE[node]
        return pltpu.make_async_remote_copy(
            src_ref=scatter_out.at[slot],
            dst_ref=scatter_in.at[slot],
            send_sem=scatter_send,
            recv_sem=scatter_recv.at[slot],
            device_id=(peer(*minus(JOINS[node], node)), feat),
            device_id_type=MESH,
        )

    def take(total, node):
        for part in PARTS.get(node, ()):
            slot = DEPARTURE[part]
            pltpu.make_async_copy(
                scatter_in.at[slot], scatter_in.at[slot], scatter_recv.at[slot]
            ).wait()
            total = total + scatter_in[slot].astype(jnp.float32)
        return total

    stops = DEPARTURES + (ROOT,)
    terms = [term(node) for node in stops[:AHEAD]]
    for i, node in enumerate(stops):
        if i + AHEAD < len(stops):
            terms.append(term(stops[i + AHEAD]))
        total = take(terms.pop(0), node)
        if node != ROOT:
            scatter_out[DEPARTURE[node]] = total.astype(jnp.bfloat16)
            scatter_copy(node).start()
    own = total

    current = u_ref[...].astype(jnp.float32)
    update = own * (math.sqrt(F) / total_samples)
    lane_of = lax.broadcasted_iota(jnp.int32, (K, 128), 1)

    def row_sum(value):
        return jnp.sum(value, axis=1, keepdims=True)

    stats = jnp.concatenate(
        [
            jnp.where(
                lane_of == 0,
                row_sum(current * current),
                jnp.where(lane_of == 1, row_sum(update * update), 0.0),
            ),
            jnp.where(lane_of == 0, row_sum(current * update), 0.0),
        ],
        axis=0,
    ).T[:2]

    def ring(i, count):
        return min(i, count - i)

    def total_over(stage, slots, me, count, device_of, distance, value):
        slots[me] = value
        for i in sorted(range(1, count), key=distance, reverse=True):
            pltpu.make_async_remote_copy(
                src_ref=slots.at[me],
                dst_ref=slots.at[me],
                send_sem=stat_send.at[stage],
                recv_sem=stat_recv.at[stage],
                device_id=device_of(i),
                device_id_type=MESH,
            ).start()
        others = slots.at[pl.ds(0, count - 1)]
        pltpu.make_async_copy(others, others, stat_recv.at[stage]).wait()
        total = slots[0]
        for i in range(1, count):
            total = total + slots[i]
        return total

    def group(i):
        return (peer(i // NF, 0), feat_peer(i % NF))

    def group_distance(i):
        return 2 * ring(i // NF, NY) + ring(i % NF, NF)

    stats = total_over(1, stat_g, y * NF + feat, NY * NF, group, group_distance, stats)
    stats = total_over(0, stat_z, z, NZ, lambda i: (peer(0, i), feat), lambda i: ring(i, NZ), stats)

    row_of = lax.broadcasted_iota(jnp.int32, (8, 128), 0)
    rows = jnp.where(row_of == 0, stats[0:1], jnp.where(row_of == 1, stats[1:2], 0.0))
    columns = jnp.concatenate([rows, jnp.zeros((120, 128), jnp.float32)], axis=0).T
    columns = columns * (1.0 / F)
    alignment = columns[K:, 0:1]
    keep = 1.0 - STEP * alignment
    squares = (
        keep * keep * columns[:K, 0:1]
        + 2.0 * STEP * keep * alignment
        + STEP * STEP * columns[:K, 1:2]
    )
    scale = lax.rsqrt(jnp.maximum(squares, 0.0) + EPSILON)
    o_ref[...] = ((keep * current + STEP * update) * scale).astype(jnp.bfloat16)

    sent = gathered.at[pl.ds(0, COPIES)]
    pltpu.make_async_copy(sent, sent, gather_send).wait()
    pltpu.make_async_copy(seven, seven, score_send).wait()
    pltpu.make_async_copy(sent, sent, scatter_send).wait()
    for stage, (slots, count) in enumerate(((stat_z, NZ), (stat_g, NY * NF))):
        others = slots.at[pl.ds(0, count - 1)]
        pltpu.make_async_copy(others, others, stat_send.at[stage]).wait()


def shards(samples, estimates):
    shaped = estimates.reshape(K, WIDTH)
    total_samples = samples.shape[0] * lax.axis_size("dp")
    bf16, f32 = jnp.bfloat16, jnp.float32
    dma = pltpu.SemaphoreType.DMA
    updated = pl.pallas_call(
        functools.partial(kernel, total_samples),
        out_shape=jax.ShapeDtypeStruct((K, WIDTH), bf16),
        in_specs=[
            pl.BlockSpec(memory_space=pl.ANY),
            pl.BlockSpec(memory_space=pl.ANY),
        ],
        out_specs=pl.BlockSpec(memory_space=pltpu.VMEM),
        scratch_shapes=[
            pltpu.VMEM((ROWS, NY * NZ * WIDTH), bf16),
            pltpu.VMEM((K, WIDTH), bf16),
            pltpu.VMEM((NY * NZ, K, WIDTH), bf16),
            pltpu.VMEM((NF, K, ROWS), bf16),
            pltpu.VMEM((COPIES, K, WIDTH), bf16),
            pltpu.VMEM((COPIES, K, WIDTH), bf16),
            pltpu.VMEM((NZ, 2, 128), f32),
            pltpu.VMEM((NY * NF, 2, 128), f32),
            dma,
            dma,
            dma,
            dma((COPIES,)),
            dma,
            dma,
            dma,
            dma((COPIES,)),
            dma((2,)),
            dma((2,)),
        ],
        compiler_params=pltpu.CompilerParams(
            collective_id=0,
            has_side_effects=True,
            vmem_limit_bytes=60 * 1024 * 1024,
        ),
        cost_estimate=pl.CostEstimate(
            flops=4 * K * ROWS * NY * NZ * WIDTH,
            bytes_accessed=2 * ROWS * NY * NZ * WIDTH,
            transcendentals=0,
        ),
    )(samples, shaped)
    return updated.reshape(K, 1, WIDTH)


def solution(mesh):
    return jax.shard_map(
        shards,
        mesh=mesh,
        in_specs=(P("dp", "feat"), P(None, "feat", "dp")),
        out_specs=P(None, "feat", "dp"),
        check_vma=False,
    )
```
